128 devices in a mesh: sec: 8 (over x, z_lo), sect: 8 (over y, core), mpo: 2 (over z_hi).
Axes of the slice: x: 4, y: 4, z: 4 (z_hi: 2, z_lo: 2; z = z_hi * 2 + z_lo), core: 2. Of those that a mesh axis runs over, the one named last changes fastest.
Arguments:
- left_env: bfloat16 [8, 18, 16, 256, 256], P('sec', 'mpo', 'sect'), may hold values from -0.375 to 0.375
- right_env: bfloat16 [8, 18, 16, 256, 256], P('sec', 'mpo', 'sect'), may hold values from -0.375 to 0.375
- onsite: float32 [8, 16, 256, 256], P('sec', 'sect'), may hold values from 0.5 to 8
- initial: float32 [8, 16, 256, 256], P('sec', 'sect'), may hold values from -6 to 6
- charges: int32 [18], P('mpo'), may hold values from 0 to 2, as said below
- kept_counts: int32 [8, 2, 16], P('sec', None, 'sect'), may hold values from 64 to 256, as said below
Outputs:
- states: float32 [8, 16, 256, 256], P('sec', 'sect')
- energies: float32 [8, 2], P('sec')
The draws below stay inside these ranges and needn't reach their ends.
Inputs may be any that keep to these rules, and one draw needn't show every extreme that they name: `charges`: each term shifts sectors by 0 to 2; some term shifts by 2. `kept_counts`: in every section and on each side some sector keeps all 256 states.
All inputs are finite; a program needn't handle non-finite values.
Results may differ from the reference program's by a relative error of at most 0.035.
Values may be sent and summed in bfloat16 or wider, within the bound.
No kernel may reach another device: no remote copies, remote signals or barrier semaphores. Data moves between devices by JAX's collectives and lax.ppermute only.
A program may use at most 128 MiB of HBM per device.

```python
import math
import jax
import jax.numpy as jnp
from jax import lax

BLOCK = 256
CHARGE_MAX = 2
ITERS = 4
TERMS = 18
SECTORS = 16
SECTIONS = 8


def draw_charges(key, part):
    key = jax.random.fold_in(key, 2)
    first_key, second_key = jax.random.split(key)
    values = jax.random.randint(first_key, (TERMS,), 0, CHARGE_MAX + 1)
    position = jax.random.randint(second_key, (), 0, TERMS)
    return jnp.where(jnp.arange(TERMS) == position, CHARGE_MAX, values).astype(jnp.int32)


def draw_kept_counts(key, part):
    key = jax.random.fold_in(key, 3)
    first_key, second_key = jax.random.split(key)
    values = jax.random.randint(first_key, (SECTIONS, 2, SECTORS), BLOCK // 4, BLOCK + 1)
    position = jax.random.randint(second_key, (SECTIONS, 2, 1), 0, SECTORS)
    sector_ids = jnp.arange(SECTORS)[None, None, :]
    return jnp.where(sector_ids == position, BLOCK, values).astype(jnp.int32)


def block_scale(rng, dims, cuts, least, top_value):
    gain, own = 1.0, jax.random.fold_in(rng, 6)
    for dim, shards_of in cuts:
        heights = jnp.exp(jax.random.uniform(jax.random.fold_in(own, dim), (shards_of,), jnp.float32, least / len(cuts), top_value / len(cuts)))
        gain = gain * jnp.repeat(heights, dims[dim] // shards_of).reshape([-1 if axis == dim else 1 for axis in range(len(dims))])
    return gain


def normal_values(own_key, extent, width, limit, pieces=(), kind=jnp.bfloat16):
    values = jax.random.normal(own_key, extent, jnp.float32) * width
    if len(pieces) > 0:
        values = block_scale(own_key, extent, pieces, -0.22, 0.18) * values
    return jnp.clip(values, min=-limit, max=limit).astype(kind)


def setup_inputs(seed: int = 0) -> dict:
    keys = jax.random.split(jax.random.key(seed), 7)
    return {
        "left_env": normal_values(keys[0], (SECTIONS, TERMS, SECTORS, BLOCK, BLOCK), BLOCK ** -0.5, 0.375, ((0, 8), (1, 2), (2, 8))),
        "right_env": normal_values(keys[1], (SECTIONS, TERMS, SECTORS, BLOCK, BLOCK), BLOCK ** -0.5, 0.375, ((0, 8), (1, 2), (2, 8))),
        "onsite": jnp.clip(jnp.exp(math.log(8.0) - 2.7725887 * jax.random.uniform(keys[2], (SECTIONS, SECTORS, BLOCK, BLOCK), jnp.float32) ** block_scale(keys[2], (SECTIONS, SECTORS, BLOCK, BLOCK), ((0, 8), (1, 8)), -0.2, 0.2)), 0.5, 8.0),
        "initial": normal_values(keys[3], (SECTIONS, SECTORS, BLOCK, BLOCK), 1.0, 6.0, ((0, 8), (1, 8)), jnp.float32),
        "charges": draw_charges(jax.random.fold_in(keys[6], 71), 0),
        "kept_counts": draw_kept_counts(jax.random.fold_in(keys[6], 71), 0),
    }


def make_mask(counts):
    index = jnp.arange(BLOCK)
    rows_ok = index[None, :, None] < counts[0][:, None, None]
    cols_ok = index[None, None, :] < counts[1][:, None, None]
    return (rows_ok & cols_ok).astype(jnp.float32)

def apply_ham(vector, left_one, right_one, charges, onsite, kept_mask):
    vector_bf = vector.astype(jnp.bfloat16)
    padded = jnp.concatenate([jnp.zeros((CHARGE_MAX, BLOCK, BLOCK), jnp.bfloat16), vector_bf], axis=0)

    def one_term(total, inputs):
        left_w, right_w, charge = inputs
        moved = lax.dynamic_slice_in_dim(padded, (CHARGE_MAX - charge).astype(jnp.int32), SECTORS, 0)
        inner_left = jnp.einsum('sij,sjk->sik', left_w.astype(jnp.float32), moved.astype(jnp.float32)).astype(jnp.bfloat16)
        forward = jnp.einsum('sik,skl->sil', inner_left.astype(jnp.float32), right_w.astype(jnp.float32))
        adjoint = jnp.einsum('sji,sjk->sik', left_w.astype(jnp.float32), vector_bf.astype(jnp.float32)).astype(jnp.bfloat16)
        backward = jnp.einsum('sik,slk->sil', adjoint.astype(jnp.float32), right_w.astype(jnp.float32))
        padded_back = jnp.concatenate([backward, jnp.zeros((CHARGE_MAX, BLOCK, BLOCK), backward.dtype)], axis=0)
        placed = lax.dynamic_slice_in_dim(padded_back, charge.astype(jnp.int32), SECTORS, 0)
        return (total + forward + placed, None)
    total, unused = lax.scan(one_term, jnp.zeros((SECTORS, BLOCK, BLOCK), jnp.float32), (left_one, right_one, charges))
    return kept_mask * (total + onsite * vector)

def davidson(start_vec, kept_mask, onsite, operator):
    vector = kept_mask * start_vec
    vector = vector / jnp.sqrt(jnp.sum(vector * vector))
    image = operator(vector)
    for iteration in range(ITERS):
        ritz_value = jnp.sum(vector * image)
        residual = image - ritz_value * vector
        correction = kept_mask * residual / jnp.maximum(jnp.abs(onsite - ritz_value), 1.0)
        correlation = jnp.sum(vector * correction)
        correction = correction - correlation * vector
        correction = correction / jnp.sqrt(jnp.sum(correction * correction))
        image_corr = operator(correction)
        cross_term = jnp.sum(vector * image_corr)
        curvature = jnp.sum(correction * image_corr)
        angle_half = 0.5 * jnp.arctan2(2.0 * cross_term, ritz_value - curvature)
        weight_x = -jnp.sin(angle_half)
        weight_t = jnp.cos(angle_half)
        flip_sign = jnp.where(weight_x < 0, -1.0, 1.0)
        vector = flip_sign * (weight_x * vector + weight_t * correction)
        image = flip_sign * (weight_x * image + weight_t * image_corr)
    return (vector, jnp.sum(vector * image))

def reference(left_env, right_env, onsite, initial, charges, kept_counts):
    masks = jax.vmap(make_mask)(kept_counts)
    scaling = math.sqrt(SECTORS * BLOCK)

    def solve_step(inputs):
        left_one, right_one, onsite_one, start_one, mask_one = inputs

        def operator(vector):
            return apply_ham(vector, left_one, right_one, charges, onsite_one, mask_one)
        return davidson(start_one, mask_one, onsite_one, operator)
    states_one, energy_one = lax.map(solve_step, (left_env, right_env, onsite, initial, masks))

    def grow(inputs):
        state_one, left_one = inputs
        frame_bf = (state_one * scaling).astype(jnp.bfloat16)
        half_env = jnp.einsum('sji,wsjk->wsik', frame_bf.astype(jnp.float32), left_one.astype(jnp.float32)).astype(jnp.bfloat16)
        return jnp.einsum('wsik,skl->wsil', half_env.astype(jnp.float32), frame_bf.astype(jnp.float32)).astype(jnp.bfloat16)
    grown = lax.map(grow, (states_one, left_env))
    left_next = jnp.concatenate([left_env[:1], grown[:-1]], axis=0)
    states_two, energy_two = lax.map(solve_step, (left_next, right_env, onsite, states_one, masks))
    return (states_two, jnp.stack([energy_one, energy_two], axis=1))
```

```python
import math

import jax
import jax.numpy as jnp
from jax import lax
from jax.experimental import pallas as pl
from jax.experimental.pallas import tpu as pltpu
from jax.sharding import PartitionSpec as P

CHARGE_MAX = 2
ITERS = 4
ROWS = 64
GROUP = ("sect", "mpo")

BF = jnp.bfloat16
F32 = jnp.float32


def shifted(x, axis, by):
    size = lax.axis_size(axis)
    pairs = [(i, i + by) for i in range(size) if 0 <= i + by < size]
    return lax.ppermute(x, axis, pairs)


def swapped(x):
    size = lax.axis_size("mpo")
    return lax.ppermute(x, "mpo", [(i, size - 1 - i) for i in range(size)])


def dot(a, b):
    return jnp.dot(a, b, preferred_element_type=F32)


def kernel_call(body, outs, operands, smem=(), scratch=(), vmem=24, flops=0):
    specs = [
        pl.BlockSpec(memory_space=pltpu.SMEM if k in smem else pltpu.VMEM)
        for k in range(len(operands))
    ]
    return pl.pallas_call(
        body,
        out_shape=outs,
        in_specs=specs,
        out_specs=[pl.BlockSpec(memory_space=pltpu.VMEM)] * len(outs),
        scratch_shapes=list(scratch),
        compiler_params=pltpu.CompilerParams(vmem_limit_bytes=vmem * 2**20),
        cost_estimate=pl.CostEstimate(flops=flops, bytes_accessed=4 * 2**20, transcendentals=0),
    )(*operands)


def field(dims, kind):
    return jax.ShapeDtypeStruct(dims, kind)


def chunk_mask(counts_ref, sector, first_row, block):
    rows = lax.broadcasted_iota(jnp.int32, (ROWS, block), 0) + first_row
    cols = lax.broadcasted_iota(jnp.int32, (ROWS, block), 1)
    return (rows < counts_ref[0, sector]) & (cols < counts_ref[1, sector])


def chunks(sec_dev, block, step, init):
    per = block // ROWS

    def body(k, carry):
        return step(k // per, pl.ds(pl.multiple_of((k % per) * ROWS, ROWS), ROWS), (k % per) * ROWS, carry)

    return lax.fori_loop(0, sec_dev * per, body, init)


def fold(values):
    rows, cols = values.shape
    return jnp.sum(values.reshape(rows // 8, 8, cols), axis=0)


def lanes(acc):
    row = jnp.sum(acc, axis=0, keepdims=True)
    total = row[:, :128]
    for k in range(1, row.shape[1] // 128):
        total = total + row[:, 128 * k : 128 * (k + 1)]
    return total


def write_rows(out_ref, rows):
    index = lax.broadcasted_iota(jnp.int32, (8, 128), 0)
    total = jnp.zeros((8, 128), F32)
    for k, row in enumerate(rows):
        if row is not None:
            total = jnp.where(index == k, jnp.broadcast_to(row, (8, 128)), total)
    out_ref[...] = total


def read_sums(scal_ref):
    total = jnp.sum(jnp.sum(scal_ref[...], axis=0), axis=1, keepdims=True)
    return [total[k : k + 1, :] for k in range(5)]


def rotation(scal_ref, theta):
    pp_ham, xp, pp, hxp, xx = read_sums(scal_ref)
    length = jnp.sqrt(pp - 2.0 * xp * xp + xp * xp * xx)
    cross = (hxp - xp * theta) / length
    curv = (pp_ham - 2.0 * xp * hxp + xp * xp * theta) / (length * length)
    two_b, diff = 2.0 * cross, theta - curv
    radius = jnp.sqrt(two_b * two_b + diff * diff)
    flat = radius == 0.0
    cos_full = jnp.where(flat, 1.0, diff / jnp.where(flat, 1.0, radius))
    sin_full = jnp.where(flat, 0.0, jnp.abs(two_b) / jnp.where(flat, 1.0, radius))
    major = jnp.sqrt(0.5 * (1.0 + jnp.abs(cos_full)))
    minor = 0.5 * sin_full / major
    weight_x = jnp.where(cos_full >= 0.0, minor, major)
    weight_t = jnp.where(cos_full >= 0.0, major, minor)
    weight_t = jnp.where(two_b > 0.0, -weight_t, weight_t)
    theta_new = (
        weight_x * weight_x * theta
        + 2.0 * weight_x * weight_t * cross
        + weight_t * weight_t * curv
    )
    coef_p = weight_t / length
    return weight_x - coef_p * xp, coef_p, theta_new


def start_kernel(counts_ref, begin_ref, u_ref, ubf_ref, dots_ref):
    sec_dev, block, _ = u_ref.shape

    def step(s, rows, first, acc):
        u = jnp.where(chunk_mask(counts_ref, s, first, block), begin_ref[s, rows, :], 0.0)
        u_ref[s, rows, :] = u
        ubf_ref[s, rows, :] = u.astype(BF)
        return acc + fold(u * u)

    acc = chunks(sec_dev, block, step, jnp.zeros((8, block), F32))
    write_rows(dots_ref, [None, None, 0.5 * lanes(acc)])


def update_kernel(first_step, *refs):
    if first_step:
        counts_ref, scal_ref, site_ref, p_ref, own_ref, other_ref, *outs = refs
    else:
        counts_ref, scal_ref, site_ref, p_ref, own_ref, other_ref, x_ref, hx_ref, st_ref, *outs = refs
    xn_ref, hxn_ref, pn_ref, pbf_ref, stn_ref, dots_ref = outs
    sec_dev, block, _ = p_ref.shape
    if first_step:
        sums = read_sums(scal_ref)
        theta = sums[0] / sums[2]
        coef_p = 1.0 / jnp.sqrt(sums[2])
        coef_x = None
    else:
        coef_x, coef_p, theta = rotation(scal_ref, st_ref[0:1, 0:1])
    stn_ref[...] = jnp.broadcast_to(theta, stn_ref.shape)

    def step(s, rows, first, acc):
        ok = chunk_mask(counts_ref, s, first, block)
        p = p_ref[s, rows, :]
        site = site_ref[s, rows, :]
        image = own_ref[s, rows, :].astype(F32) + other_ref[s, rows, :].astype(F32) + site * p
        image = jnp.where(ok, image, 0.0)
        if first_step:
            x, hx = coef_p * p, coef_p * image
        else:
            x = coef_x * x_ref[s, rows, :] + coef_p * p
            hx = coef_x * hx_ref[s, rows, :] + coef_p * image
        residual = hx - theta * x
        new = jnp.where(ok, residual / jnp.maximum(jnp.abs(site - theta), 1.0), 0.0)
        xn_ref[s, rows, :] = x
        hxn_ref[s, rows, :] = hx
        pn_ref[s, rows, :] = new
        pbf_ref[s, rows, :] = new.astype(BF)
        return (
            acc[0] + fold(x * new),
            acc[1] + fold(new * new),
            acc[2] + fold(hx * new),
            acc[3] + fold(x * x),
        )

    zero = jnp.zeros((8, block), F32)
    acc = chunks(sec_dev, block, step, (zero, zero, zero, zero))
    write_rows(dots_ref, [None] + [0.5 * lanes(a) for a in acc])


def finish_kernel(scal_ref, st_ref, x_ref, p_ref, xn_ref, xbf_ref, stn_ref, dots_ref):
    sec_dev, block, _ = p_ref.shape
    coef_x, coef_p, theta = rotation(scal_ref, st_ref[0:1, 0:1])
    stn_ref[...] = jnp.broadcast_to(theta, stn_ref.shape)

    def step(s, rows, first, acc):
        x = coef_x * x_ref[s, rows, :] + coef_p * p_ref[s, rows, :]
        xn_ref[s, rows, :] = x
        xbf_ref[s, rows, :] = x.astype(BF)
        return acc + fold(x * x)

    acc = chunks(sec_dev, block, step, jnp.zeros((8, block), F32))
    write_rows(dots_ref, [None, None, 0.5 * lanes(acc)])


def adjoint_kernel(charges_ref, pbf_ref, left_ref, right_ref, own_ref, down_ref, acc_ref):
    terms, sec_dev, block, _ = left_ref.shape
    acc_ref[...] = jnp.zeros_like(acc_ref)
    for s in range(sec_dev):
        turned = pbf_ref[s].T
        for w in range(terms):
            adjoint = dot(turned, left_ref[w, s]).astype(BF)
            target = s + CHARGE_MAX - charges_ref[w]
            acc_ref[target] += dot(right_ref[w, s], adjoint)
    for s in range(sec_dev):
        down_ref[s] = acc_ref[s].T.astype(BF)
        own_ref[s] = acc_ref[CHARGE_MAX + s].T


def forward_kernel(
    charges_ref, rim_ref, pbf_ref, left_ref, right_ref, p_ref, site_ref, dots_ref, *rest
):
    terms, sec_dev, block, _ = left_ref.shape
    if len(rest) == 4:
        own_ref, part_ref, sums_ref, ext_ref = rest
    else:
        sums_ref, ext_ref = rest
    ext_ref[:CHARGE_MAX] = rim_ref[...]
    ext_ref[CHARGE_MAX:] = pbf_ref[...]
    total = jnp.zeros((8, block), F32)
    for s in range(sec_dev):
        out = jnp.zeros((block, block), F32)
        for w in range(terms):
            moved = ext_ref[s + CHARGE_MAX - charges_ref[w]]
            inner = dot(left_ref[w, s], moved).astype(BF)
            out = out + dot(inner, right_ref[w, s])
        p = p_ref[s]
        total = total + fold(p * (2.0 * out + 0.5 * site_ref[s] * p))
        if len(rest) == 4:
            part_ref[s] = out + own_ref[s]
    index = lax.broadcasted_iota(jnp.int32, (8, 128), 0)
    sums = jnp.where(index == 0, jnp.broadcast_to(lanes(total), (8, 128)), dots_ref[...])
    sums_ref[...] = jnp.broadcast_to(sums[None], sums_ref.shape)


def grow_kernel(place_ref, frame_ref, before_ref, left_ref, out_ref):
    terms, sec_dev, block, _ = left_ref.shape
    scale = math.sqrt(place_ref_sectors(frame_ref) * block)

    @pl.when(place_ref[0] == 0)
    def _():
        out_ref[...] = left_ref[...]

    @pl.when(place_ref[0] != 0)
    def _():
        for s in range(sec_dev):
            frame = (frame_ref[s].astype(F32) * scale).astype(BF)
            turned = frame.T
            for w in range(terms):
                half = dot(turned, before_ref[w, s]).astype(BF)
                out_ref[w, s] = dot(half, frame).astype(BF)


def place_ref_sectors(frame_ref):
    return frame_ref.shape[0] * lax.axis_size("sect")


def on_device(left_env, right_env, onsite, initial, charges, kept_counts):
    left_one, right_one = left_env[0], right_env[0]
    site, begin, counts = onsite[0], initial[0], kept_counts[0]
    terms, sec_dev, block, _ = left_one.shape
    dims = (sec_dev, block, block)
    full, half, rows = field(dims, F32), field(dims, BF), field((8, 128), F32)
    size = lax.axis_size("sect") * lax.axis_size("mpo")
    spread = field((size, 8, 128), F32)
    work = 4 * terms * sec_dev * block**3
    place = lax.axis_index("sec").astype(jnp.int32).reshape(1)
    ext = pltpu.VMEM((sec_dev + CHARGE_MAX, block, block), BF)
    ext_sum = pltpu.VMEM((sec_dev + CHARGE_MAX, block, block), F32)

    left_before = shifted(left_one, "sec", 1)

    def exchange(sums):
        return lax.all_to_all(sums, GROUP, 0, 0)

    def apply(p, pbf, left_use, dots):
        rim = shifted(pbf, "sect", 1)
        own, down = kernel_call(
            adjoint_kernel, [full, half], [charges, pbf, left_use, right_one],
            smem=(0,), scratch=[ext_sum], flops=work)
        upper = shifted(down, "sect", -1)
        part, sums = kernel_call(
            forward_kernel, [full, spread],
            [charges, rim, pbf, left_use, right_one, p, site, dots, own],
            smem=(0,), scratch=[ext], flops=work)
        own = (part + upper.astype(F32)).astype(BF)
        own, sums = lax.optimization_barrier((own, sums))
        other = swapped(own)
        return own, other, exchange(sums)

    def davidson(u, ubf, dots, left_use):
        own, other, scal = apply(u, ubf, left_use, dots)
        new = [full, full, full, half, rows, rows]
        x, hx, p, pbf, st, dots = kernel_call(
            lambda *refs: update_kernel(True, *refs), new,
            [counts, scal, site, u, own, other], smem=(0,))
        for _ in range(ITERS - 1):
            own, other, scal = apply(p, pbf, left_use, dots)
            x, hx, p, pbf, st, dots = kernel_call(
                lambda *refs: update_kernel(False, *refs), new,
                [counts, scal, site, p, own, other, x, hx, st], smem=(0,))
        rim = shifted(pbf, "sect", 1)
        (sums,) = kernel_call(
            forward_kernel, [spread],
            [charges, rim, pbf, left_use, right_one, p, site, dots],
            smem=(0,), scratch=[ext], flops=work)
        return kernel_call(
            finish_kernel, [full, half, rows, rows], [exchange(sums), st, x, p])

    u, ubf, dots = kernel_call(start_kernel, [full, half, rows], [counts, begin], smem=(0,))
    x, xbf, st_one, dots = davidson(u, ubf, dots, left_one)
    frame = shifted(xbf, "sec", 1)
    (left_next,) = kernel_call(
        grow_kernel, [field(left_one.shape, BF)], [place, frame, left_before, left_one],
        smem=(0,), flops=work)
    x, _, st_two, _ = davidson(x, xbf, dots, left_next)
    return x[None], jnp.stack([st_one[0, 0], st_two[0, 0]])[None]


def solution(mesh):
    return jax.shard_map(
        on_device,
        mesh=mesh,
        in_specs=(
            P("sec", "mpo", "sect", None, None),
            P("sec", "mpo", "sect", None, None),
            P("sec", "sect", None, None),
            P("sec", "sect", None, None),
            P("mpo"),
            P("sec", None, "sect"),
        ),
        out_specs=(P("sec", "sect", None, None), P("sec", None)),
        check_vma=False,
    )
```

```python
import math

import jax
import jax.numpy as jnp
from jax import lax
from jax.experimental import pallas as pl
from jax.experimental.pallas import tpu as pltpu
from jax.sharding import PartitionSpec as P

CHARGE_MAX = 2
ITERS = 4
ROWS = 64

BF = jnp.bfloat16
F32 = jnp.float32


def shifted(x, axis, by):
    size = lax.axis_size(axis)
    pairs = [(i, i + by) for i in range(size) if 0 <= i + by < size]
    return lax.ppermute(x, axis, pairs)


def swapped(x, axis, mask):
    return lax.ppermute(x, axis, [(i, i ^ mask) for i in range(lax.axis_size(axis))])


def dot(a, b):
    return jnp.dot(a, b, preferred_element_type=F32)


def kernel_call(body, outs, operands, smem=(), hbm=0, scratch=(), vmem=12, flops=0):
    spaces = [pltpu.SMEM if k in smem else pltpu.VMEM for k in range(len(operands))]
    if hbm:
        spaces[-hbm:] = [pltpu.HBM] * hbm
    return pl.pallas_call(
        body,
        out_shape=outs,
        in_specs=[pl.BlockSpec(memory_space=space) for space in spaces],
        out_specs=[pl.BlockSpec(memory_space=pltpu.VMEM)] * len(outs),
        scratch_shapes=list(scratch),
        compiler_params=pltpu.CompilerParams(vmem_limit_bytes=vmem * 2**20),
        cost_estimate=pl.CostEstimate(flops=flops, bytes_accessed=4 * 2**20, transcendentals=0),
    )(*operands)


def field(dims, kind):
    return jax.ShapeDtypeStruct(dims, kind)


def chunk_mask(counts_ref, sector, first_row, block):
    rows = lax.broadcasted_iota(jnp.int32, (ROWS, block), 0) + first_row
    cols = lax.broadcasted_iota(jnp.int32, (ROWS, block), 1)
    return (rows < counts_ref[0, sector]) & (cols < counts_ref[1, sector])


def chunks(sec_dev, block, step, init):
    per = block // ROWS

    def body(k, carry):
        return step(k // per, pl.ds(pl.multiple_of((k % per) * ROWS, ROWS), ROWS), (k % per) * ROWS, carry)

    return lax.fori_loop(0, sec_dev * per, body, init)


def fold(values):
    rows, cols = values.shape
    return jnp.sum(values.reshape(rows // 8, 8, cols), axis=0)


def lanes(acc):
    row = jnp.sum(acc, axis=0, keepdims=True)
    total = row[:, :128]
    for k in range(1, row.shape[1] // 128):
        total = total + row[:, 128 * k : 128 * (k + 1)]
    return total


def write_rows(out_ref, rows):
    index = lax.broadcasted_iota(jnp.int32, (8, 128), 0)
    total = jnp.zeros((8, 128), F32)
    for k, row in enumerate(rows):
        if row is not None:
            total = jnp.where(index == k, jnp.broadcast_to(row, (8, 128)), total)
    out_ref[...] = total


def read_sums(sums_ref):
    total = jnp.sum(jnp.sum(sums_ref[...], axis=0), axis=1, keepdims=True)
    return [total[k : k + 1, :] for k in range(5)]


def rotation(sums, theta):
    pp_ham, xp, pp, hxp, xx = sums
    length = jnp.sqrt(pp - 2.0 * xp * xp + xp * xp * xx)
    cross = (hxp - xp * theta) / length
    curv = (pp_ham - 2.0 * xp * hxp + xp * xp * theta) / (length * length)
    two_b, diff = 2.0 * cross, theta - curv
    radius = jnp.sqrt(two_b * two_b + diff * diff)
    flat = radius == 0.0
    cos_full = jnp.where(flat, 1.0, diff / jnp.where(flat, 1.0, radius))
    sin_full = jnp.where(flat, 0.0, jnp.abs(two_b) / jnp.where(flat, 1.0, radius))
    major = jnp.sqrt(0.5 * (1.0 + jnp.abs(cos_full)))
    minor = 0.5 * sin_full / major
    weight_x = jnp.where(cos_full >= 0.0, minor, major)
    weight_t = jnp.where(cos_full >= 0.0, major, minor)
    weight_t = jnp.where(two_b > 0.0, -weight_t, weight_t)
    theta_new = (
        weight_x * weight_x * theta
        + 2.0 * weight_x * weight_t * cross
        + weight_t * weight_t * curv
    )
    coef_p = weight_t / length
    return weight_x - coef_p * xp, coef_p, theta_new


def start_kernel(counts_ref, begin_ref, u_ref, ubf_ref, mask_ref, dots_ref):
    sec_dev, block, _ = u_ref.shape

    def step(s, rows, first, acc):
        mask = jnp.where(chunk_mask(counts_ref, s, first, block), 1.0, 0.0)
        u = mask * begin_ref[s, rows, :]
        mask_ref[s, rows, :] = mask
        u_ref[s, rows, :] = u
        ubf_ref[s, rows, :] = u.astype(BF)
        return acc + fold(u * u)

    acc = chunks(sec_dev, block, step, jnp.zeros((8, block), F32))
    write_rows(dots_ref, [None, None, 0.5 * lanes(acc)])


def update_kernel(first_step, *refs):
    if first_step:
        sums_ref, mask_ref, site_ref, p_ref, own_ref, other_ref, *outs = refs
    else:
        sums_ref, mask_ref, site_ref, p_ref, own_ref, other_ref, x_ref, hx_ref, st_ref, *outs = refs
    xn_ref, hxn_ref, pn_ref, pbf_ref, stn_ref, dots_ref = outs
    sec_dev, block, _ = p_ref.shape
    sums = read_sums(sums_ref)
    if first_step:
        theta = sums[0] / sums[2]
        coef_p = 1.0 / jnp.sqrt(sums[2])
    else:
        coef_x, coef_p, theta = rotation(sums, st_ref[0:1, 0:1])
    stn_ref[...] = jnp.broadcast_to(theta, stn_ref.shape)

    def step(s, rows, first, acc):
        p = p_ref[s, rows, :]
        site = site_ref[s, rows, :]
        image = own_ref[s, rows, :].astype(F32) + other_ref[s, rows, :].astype(F32) + site * p
        image = mask_ref[s, rows, :] * image
        if first_step:
            x, hx = coef_p * p, coef_p * image
        else:
            x = coef_x * x_ref[s, rows, :] + coef_p * p
            hx = coef_x * hx_ref[s, rows, :] + coef_p * image
        new = (hx - theta * x) / jnp.maximum(jnp.abs(site - theta), 1.0)
        xn_ref[s, rows, :] = x
        hxn_ref[s, rows, :] = hx
        pn_ref[s, rows, :] = new
        pbf_ref[s, rows, :] = new.astype(BF)
        return (
            acc[0] + fold(x * new),
            acc[1] + fold(new * new),
            acc[2] + fold(hx * new),
            acc[3] + fold(x * x),
        )

    zero = jnp.zeros((8, block), F32)
    acc = chunks(sec_dev, block, step, (zero, zero, zero, zero))
    write_rows(dots_ref, [None] + [0.5 * lanes(a) for a in acc])


def finish_kernel(sums_ref, st_ref, x_ref, p_ref, xn_ref, xbf_ref, stn_ref, dots_ref):
    sec_dev, block, _ = p_ref.shape
    coef_x, coef_p, theta = rotation(read_sums(sums_ref), st_ref[0:1, 0:1])
    stn_ref[...] = jnp.broadcast_to(theta, stn_ref.shape)

    def step(s, rows, first, acc):
        x = coef_x * x_ref[s, rows, :] + coef_p * p_ref[s, rows, :]
        xn_ref[s, rows, :] = x
        xbf_ref[s, rows, :] = x.astype(BF)
        return acc + fold(x * x)

    acc = chunks(sec_dev, block, step, jnp.zeros((8, block), F32))
    write_rows(dots_ref, [None, None, 0.5 * lanes(acc)])


def adjoint_kernel(
    charges_ref, pbf_ref, p_ref, site_ref, dots_ref, left_ref, right_ref,
    own_ref, down_ref, sums_ref, acc_ref,
):
    terms, sec_dev, block, _ = left_ref.shape
    acc_ref[...] = jnp.zeros_like(acc_ref)
    for s in range(sec_dev):
        turned = pbf_ref[s].T
        for w in range(terms):
            adjoint = dot(turned, left_ref[w, s]).astype(BF)
            target = s + CHARGE_MAX - charges_ref[w]
            acc_ref[target] += dot(right_ref[w, s], adjoint)
    total = jnp.zeros((8, block), F32)
    for s in range(sec_dev):
        down_ref[s] = acc_ref[s].T.astype(BF)
        own = acc_ref[CHARGE_MAX + s].T
        own_ref[s] = own
        p = p_ref[s]
        total = total + fold(p * (2.0 * own + 0.5 * site_ref[s] * p))
    index = lax.broadcasted_iota(jnp.int32, (8, 128), 0)
    row = jnp.broadcast_to(lanes(total), (8, 128))
    sums_ref[...] = jnp.where(index == 0, row, dots_ref[...])


def cross_kernel(rim_ref, down_ref, dots_ref, sums_ref):
    sec_dev, block, _ = rim_ref.shape

    def step(s, rows, first, acc):
        return acc + fold(rim_ref[s, rows, :].astype(F32) * down_ref[s, rows, :].astype(F32))

    acc = chunks(sec_dev, block, step, jnp.zeros((8, block), F32))
    index = lax.broadcasted_iota(jnp.int32, (8, 128), 0)
    row = jnp.broadcast_to(2.0 * lanes(acc), (8, 128))
    sums_ref[...] = dots_ref[...] + jnp.where(index == 0, row, 0.0)


def forward_kernel(
    first, charges_ref, rim_ref, pbf_ref, left_ref, right_ref, own_ref, after_ref,
    part_ref, *refs,
):
    *chunk_refs, ext_ref = refs
    terms, sec_dev, block, _ = left_ref.shape
    for chunk_ref in chunk_refs:
        chunk_ref[...] = left_ref[first : first + chunk_ref.shape[0]]
        first += chunk_ref.shape[0]
    ext_ref[:CHARGE_MAX] = rim_ref[...]
    ext_ref[CHARGE_MAX:] = pbf_ref[...]
    for s in range(sec_dev):
        out = own_ref[s]
        for w in range(terms):
            moved = ext_ref[s + CHARGE_MAX - charges_ref[w]]
            inner = dot(left_ref[w, s], moved).astype(BF)
            out = out + dot(inner, right_ref[w, s])
        part_ref[s] = out


def grow_kernel(sectors, place_ref, frame_ref, left_ref, *refs):
    *before_refs, out_ref = refs
    terms, sec_dev, block, _ = left_ref.shape
    scale = math.sqrt(sectors * block)
    slots = [ref.at[k] for ref in before_refs for k in range(ref.shape[0])]

    @pl.when(place_ref[0] == 0)
    def _():
        out_ref[...] = left_ref[...]

    @pl.when(place_ref[0] != 0)
    def _():
        for s in range(sec_dev):
            frame = (frame_ref[s].astype(F32) * scale).astype(BF)
            turned = frame.T
            for w in range(terms):
                half = dot(turned, slots[w][s]).astype(BF)
                out_ref[w, s] = dot(half, frame).astype(BF)


def copy_kernel(in_ref, out_ref):
    out_ref[...] = in_ref[...]


def on_device(left_env, right_env, onsite, initial, charges, kept_counts):
    left_one, right_one = left_env[0], right_env[0]
    site, begin, counts = onsite[0], initial[0], kept_counts[0]
    terms, sec_dev, block, _ = left_one.shape
    dims = (sec_dev, block, block)
    full, half, rows = field(dims, F32), field(dims, BF), field((8, 128), F32)
    work = 4 * terms * sec_dev * block**3
    place = lax.axis_index("sec").astype(jnp.int32).reshape(1)
    peers = lax.axis_size("sect")
    sectors = sec_dev * peers
    ext = pltpu.VMEM((sec_dev + CHARGE_MAX, block, block), BF)
    ext_sum = pltpu.VMEM((sec_dev + CHARGE_MAX, block, block), F32)
    before = []
    taken = [0]

    def exchange(sums):
        return lax.all_to_all(jnp.broadcast_to(sums, (peers, 8, 128)), "sect", 0, 0)

    def backward(p, pbf, envs, dots):
        rim = shifted(pbf, "sect", 1)
        own, down, dots = kernel_call(
            adjoint_kernel, [full, half, rows],
            [charges, pbf, p, site, dots, *envs], smem=(0,), scratch=[ext_sum], flops=work)
        (sums,) = kernel_call(cross_kernel, [rows], [rim, down, dots])
        return rim, own, down, sums

    def apply(p, pbf, envs, dots, moving, counts):
        rim, own, down, sums = backward(p, pbf, envs, dots)
        across = swapped(sums, "mpo", 1)
        upper = shifted(down, "sect", -1)
        chunks = [field((count, *dims), BF) for count in counts]
        first = taken[0]
        taken[0] += sum(counts)
        part, *chunks = kernel_call(
            lambda *refs: forward_kernel(first, *refs), [full, *chunks],
            [charges, rim, pbf, *envs, own, sums],
            smem=(0,), scratch=[ext], flops=work)
        own = (part + upper.astype(F32)).astype(BF)
        own, sums, moving, chunks = lax.optimization_barrier((own, sums + across, moving, chunks))
        before.extend(moving)
        moving = [shifted(c, "sec", 1) for c in chunks[:1]]
        return own, swapped(own, "mpo", 1), exchange(sums), moving, chunks[1:]

    def davidson(u, ubf, dots, envs, plan, moving):
        new = [full, full, full, half, rows, rows]
        own, other, sums, moving, late = apply(u, ubf, envs, dots, moving, plan[0])
        x, hx, p, pbf, st, dots = kernel_call(
            lambda *refs: update_kernel(True, *refs), new,
            [sums, mask, site, u, own, other])
        for turn in range(ITERS - 1):
            own, other, sums, moving, late = apply(p, pbf, envs, dots, moving, plan[1 + turn])
            x, hx, p, pbf, st, dots = kernel_call(
                lambda *refs: update_kernel(False, *refs), new,
                [sums, mask, site, p, own, other, x, hx, st])
        before.extend(moving)
        sums = backward(p, pbf, envs, dots)[3]
        sums = sums + swapped(sums, "mpo", 1)
        late, sums = lax.optimization_barrier((late, sums))
        before.extend(shifted(c, "sec", 1) for c in late)
        return kernel_call(
            finish_kernel, [full, half, rows, rows], [exchange(sums), st, x, p])

    u, ubf, mask, dots = kernel_call(start_kernel, [full, half, full, rows], [counts, begin], smem=(0,))
    (left_held,) = kernel_call(copy_kernel, [field(left_one.shape, BF)], [left_one])
    taken[0] = 0
    moving = [shifted(left_one[:0], "sec", 1)] if 0 else []
    x, xbf, st_one, dots = davidson(u, ubf, dots, (left_held, right_one), [(2,), (2,), (2,), (1, 2)], moving)
    frame = shifted(xbf, "sec", 1)
    (left_next,) = kernel_call(
        lambda *refs: grow_kernel(sectors, *refs), [field(left_one.shape, BF)],
        [place, frame, left_held, *before], smem=(0,), flops=work)
    x, _, st_two, _ = davidson(x, xbf, dots, (left_next, right_one), [()] * ITERS, [])
    return x[None], jnp.stack([st_one[0, 0], st_two[0, 0]])[None]


def solution(mesh):
    return jax.shard_map(
        on_device,
        mesh=mesh,
        in_specs=(
            P("sec", "mpo", "sect", None, None),
            P("sec", "mpo", "sect", None, None),
            P("sec", "sect", None, None),
            P("sec", "sect", None, None),
            P("mpo"),
            P("sec", None, "sect"),
        ),
        out_specs=(P("sec", "sect", None, None), P("sec", None)),
        check_vma=False,
    )
```

```python
import math

import jax
import jax.numpy as jnp
from jax import lax
from jax.experimental import pallas as pl
from jax.experimental.pallas import tpu as pltpu
from jax.sharding import PartitionSpec as P

CHARGE_MAX = 2
ITERS = 4
ROWS = 64

BF = jnp.bfloat16
F32 = jnp.float32


def shifted(x, axis, by):
    size = lax.axis_size(axis)
    pairs = [(i, i + by) for i in range(size) if 0 <= i + by < size]
    return lax.ppermute(x, axis, pairs)


def swapped(x, axis, mask):
    return lax.ppermute(x, axis, [(i, i ^ mask) for i in range(lax.axis_size(axis))])


def dot(a, b):
    return jnp.dot(a, b, preferred_element_type=F32)


def kernel_call(body, outs, operands, smem=(), scratch=(), vmem=12, flops=0, alias=None):
    spaces = [pltpu.SMEM if k in smem else pltpu.VMEM for k in range(len(operands))]
    return pl.pallas_call(
        body,
        out_shape=outs,
        in_specs=[pl.BlockSpec(memory_space=space) for space in spaces],
        out_specs=[pl.BlockSpec(memory_space=pltpu.VMEM)] * len(outs),
        scratch_shapes=list(scratch),
        input_output_aliases=alias or {},
        compiler_params=pltpu.CompilerParams(vmem_limit_bytes=vmem * 2**20),
        cost_estimate=pl.CostEstimate(flops=flops, bytes_accessed=4 * 2**20, transcendentals=0),
    )(*operands)


def field(dims, kind):
    return jax.ShapeDtypeStruct(dims, kind)


def chunk_mask(counts_ref, sector, first_row, block):
    rows = lax.broadcasted_iota(jnp.int32, (ROWS, block), 0) + first_row
    cols = lax.broadcasted_iota(jnp.int32, (ROWS, block), 1)
    return (rows < counts_ref[0, sector]) & (cols < counts_ref[1, sector])


def chunks(sec_dev, block, step, init):
    per = block // ROWS

    def body(k, carry):
        return step(k // per, pl.ds(pl.multiple_of((k % per) * ROWS, ROWS), ROWS), (k % per) * ROWS, carry)

    return lax.fori_loop(0, sec_dev * per, body, init)


def fold(values):
    rows, cols = values.shape
    return jnp.sum(values.reshape(rows // 8, 8, cols), axis=0)


def lanes(acc):
    row = jnp.sum(acc, axis=0, keepdims=True)
    total = row[:, :128]
    for k in range(1, row.shape[1] // 128):
        total = total + row[:, 128 * k : 128 * (k + 1)]
    return total


def write_rows(out_ref, rows):
    index = lax.broadcasted_iota(jnp.int32, (8, 128), 0)
    total = jnp.zeros((8, 128), F32)
    for k, row in enumerate(rows):
        if row is not None:
            total = jnp.where(index == k, jnp.broadcast_to(row, (8, 128)), total)
    out_ref[...] = total


def read_sums(sums_ref):
    total = jnp.sum(jnp.sum(sums_ref[...], axis=0), axis=1, keepdims=True)
    return [total[k : k + 1, :] for k in range(5)]


def rotation(sums, theta):
    pp_ham, xp, pp, hxp, xx = sums
    length = jnp.sqrt(pp - 2.0 * xp * xp + xp * xp * xx)
    cross = (hxp - xp * theta) / length
    curv = (pp_ham - 2.0 * xp * hxp + xp * xp * theta) / (length * length)
    two_b, diff = 2.0 * cross, theta - curv
    radius = jnp.sqrt(two_b * two_b + diff * diff)
    flat = radius == 0.0
    cos_full = jnp.where(flat, 1.0, diff / jnp.where(flat, 1.0, radius))
    sin_full = jnp.where(flat, 0.0, jnp.abs(two_b) / jnp.where(flat, 1.0, radius))
    major = jnp.sqrt(0.5 * (1.0 + jnp.abs(cos_full)))
    minor = 0.5 * sin_full / major
    weight_x = jnp.where(cos_full >= 0.0, minor, major)
    weight_t = jnp.where(cos_full >= 0.0, major, minor)
    weight_t = jnp.where(two_b > 0.0, -weight_t, weight_t)
    theta_new = (
        weight_x * weight_x * theta
        + 2.0 * weight_x * weight_t * cross
        + weight_t * weight_t * curv
    )
    coef_p = weight_t / length
    return weight_x - coef_p * xp, coef_p, theta_new


def start_kernel(counts_ref, begin_ref, site_ref, u_ref, ubf_ref, signed_ref, dots_ref):
    sec_dev, block, _ = u_ref.shape

    def step(s, rows, first, acc):
        kept = chunk_mask(counts_ref, s, first, block)
        site = site_ref[s, rows, :]
        u = jnp.where(kept, begin_ref[s, rows, :], 0.0)
        signed_ref[s, rows, :] = jnp.where(kept, site, -site)
        u_ref[s, rows, :] = u
        ubf_ref[s, rows, :] = u.astype(BF)
        return acc + fold(u * u)

    acc = chunks(sec_dev, block, step, jnp.zeros((8, block), F32))
    write_rows(dots_ref, [None, None, 0.5 * lanes(acc)])


def update_kernel(first_step, last_step, *refs):
    if first_step:
        sums_ref, site_ref, p_ref, own_ref, other_ref, *outs = refs
    else:
        sums_ref, site_ref, p_ref, own_ref, other_ref, x_ref, hx_ref, st_ref, *outs = refs
    xn_ref, pn_ref, pbf_ref, stn_ref, dots_ref, *hxn_ref = outs
    sec_dev, block, _ = p_ref.shape
    sums = read_sums(sums_ref)
    if first_step:
        theta = sums[0] / sums[2]
        coef_p = 1.0 / jnp.sqrt(sums[2])
    else:
        coef_x, coef_p, theta = rotation(sums, st_ref[0:1, 0:1])
    stn_ref[...] = jnp.broadcast_to(theta, stn_ref.shape)

    def step(s, rows, first, acc):
        p = p_ref[s, rows, :]
        site = site_ref[s, rows, :]
        image = own_ref[s, rows, :].astype(F32) + other_ref[s, rows, :].astype(F32) + site * p
        image = jnp.where(site > 0.0, image, 0.0)
        if first_step:
            x, hx = coef_p * p, coef_p * image
        else:
            x = coef_x * x_ref[s, rows, :] + coef_p * p
            hx = coef_x * hx_ref[s, rows, :] + coef_p * image
        new = (hx - theta * x) / jnp.maximum(jnp.abs(site - theta), 1.0)
        xn_ref[s, rows, :] = x
        if not last_step:
            hxn_ref[0][s, rows, :] = hx
        pn_ref[s, rows, :] = new
        pbf_ref[s, rows, :] = new.astype(BF)
        return (
            acc[0] + fold(x * new),
            acc[1] + fold(new * new),
            acc[2] + fold(hx * new),
            acc[3] + fold(x * x),
        )

    zero = jnp.zeros((8, block), F32)
    acc = chunks(sec_dev, block, step, (zero, zero, zero, zero))
    write_rows(dots_ref, [None] + [0.5 * lanes(a) for a in acc])


def finish_kernel(last, sums_ref, st_ref, x_ref, p_ref, *refs):
    if last:
        st_one_ref, xn_ref, stn_ref = refs
    else:
        xn_ref, xbf_ref, stn_ref, dots_ref = refs
    sec_dev, block, _ = p_ref.shape
    coef_x, coef_p, theta = rotation(read_sums(sums_ref), st_ref[0:1, 0:1])
    if last:
        stn_ref[...] = jnp.concatenate([st_one_ref[0:1, 0:1], theta], axis=1)
    else:
        stn_ref[...] = jnp.broadcast_to(theta, stn_ref.shape)

    def step(s, rows, first, acc):
        x = coef_x * x_ref[s, rows, :] + coef_p * p_ref[s, rows, :]
        xn_ref[s, rows, :] = x
        if not last:
            xbf_ref[s, rows, :] = x.astype(BF)
            acc = acc + fold(x * x)
        return acc

    acc = chunks(sec_dev, block, step, jnp.zeros((8, block), F32))
    if not last:
        write_rows(dots_ref, [None, None, 0.5 * lanes(acc)])


def adjoint_kernel(
    charges_ref, pbf_ref, p_ref, site_ref, dots_ref, left_ref, right_ref, down_ref, sums_ref, *refs
):
    *own_ref, acc_ref = refs
    terms, sec_dev, block, _ = left_ref.shape
    acc_ref[...] = jnp.zeros_like(acc_ref)
    for s in range(sec_dev):
        turned = pbf_ref[s].T
        for w in range(terms):
            adjoint = dot(turned, left_ref[w, s]).astype(BF)
            target = s + CHARGE_MAX - charges_ref[w]
            acc_ref[target] += dot(right_ref[w, s], adjoint)
    total = jnp.zeros((8, block), F32)
    for s in range(sec_dev):
        down_ref[s] = acc_ref[s].T.astype(BF)
        own = acc_ref[CHARGE_MAX + s].T
        if own_ref:
            own_ref[0][s] = own
        p = p_ref[s]
        total = total + fold(p * (2.0 * own + 0.5 * site_ref[s] * p))
    index = lax.broadcasted_iota(jnp.int32, (8, 128), 0)
    row = jnp.broadcast_to(lanes(total), (8, 128))
    sums_ref[...] = jnp.where(index == 0, row, dots_ref[...])


def cross_kernel(rim_ref, down_ref, dots_ref, sums_ref):
    sec_dev, block, _ = rim_ref.shape

    def step(s, rows, first, acc):
        return acc + fold(rim_ref[s, rows, :].astype(F32) * down_ref[s, rows, :].astype(F32))

    acc = chunks(sec_dev, block, step, jnp.zeros((8, block), F32))
    index = lax.broadcasted_iota(jnp.int32, (8, 128), 0)
    row = jnp.broadcast_to(2.0 * lanes(acc), (8, 128))
    sums_ref[...] = dots_ref[...] + jnp.where(index == 0, row, 0.0)


def forward_kernel(
    first, charges_ref, rim_ref, pbf_ref, left_ref, right_ref, own_ref, after_ref,
    part_ref, *refs,
):
    *chunk_refs, ext_ref = refs
    terms, sec_dev, block, _ = left_ref.shape
    for chunk_ref in chunk_refs:
        chunk_ref[...] = left_ref[first : first + chunk_ref.shape[0]]
        first += chunk_ref.shape[0]
    ext_ref[:CHARGE_MAX] = rim_ref[...]
    ext_ref[CHARGE_MAX:] = pbf_ref[...]
    for s in range(sec_dev):
        out = own_ref[s]
        for w in range(terms):
            moved = ext_ref[s + CHARGE_MAX - charges_ref[w]]
            inner = dot(left_ref[w, s], moved).astype(BF)
            out = out + dot(inner, right_ref[w, s])
        part_ref[s] = out


def gather_kernel(*refs):
    left_ref, *before_refs, next_ref, held_ref = refs
    next_ref[...] = left_ref[...]
    first = 0
    for ref in before_refs:
        held_ref[first : first + ref.shape[0]] = ref[...]
        first += ref.shape[0]


def grow_kernel(sectors, place_ref, frame_ref, next_ref, *refs):
    *before_refs, out_ref = refs
    _, sec_dev, block, _ = next_ref.shape
    scale = math.sqrt(sectors * block)

    @pl.when(place_ref[0] == 0)
    def _():
        out_ref[...] = next_ref[...]

    slots = [ref.at[k] for ref in before_refs for k in range(ref.shape[0])]

    @pl.when(place_ref[0] != 0)
    def _():
        for s in range(sec_dev):
            frame = (frame_ref[s].astype(F32) * scale).astype(BF)
            turned = frame.T
            for w, slot in enumerate(slots):
                half = dot(turned, slot[s]).astype(BF)
                out_ref[w, s] = dot(half, frame).astype(BF)


def copy_kernel(in_ref, out_ref):
    out_ref[...] = in_ref[...]


def on_device(left_env, right_env, onsite, initial, charges, kept_counts):
    left_one, right_one = left_env[0], right_env[0]
    begin, counts = initial[0], kept_counts[0]
    terms, sec_dev, block, _ = left_one.shape
    dims = (sec_dev, block, block)
    full, half, rows = field(dims, F32), field(dims, BF), field((8, 128), F32)
    work = 4 * terms * sec_dev * block**3
    place = lax.axis_index("sec").astype(jnp.int32).reshape(1)
    peers = lax.axis_size("sect")
    sectors = sec_dev * peers
    ext = pltpu.VMEM((sec_dev + CHARGE_MAX, block, block), BF)
    ext_sum = pltpu.VMEM((sec_dev + CHARGE_MAX, block, block), F32)
    before = []
    taken = [0]

    def exchange(sums, axes="sect"):
        count = math.prod(lax.axis_size(axis) for axis in ([axes] if axes == "sect" else axes))
        return lax.all_to_all(jnp.broadcast_to(sums, (count, 8, 128)), axes, 0, 0)

    def backward(p, pbf, envs, dots, final=False):
        rim = shifted(pbf, "sect", 1)
        down, dots, *own = kernel_call(
            adjoint_kernel, [half, rows] + ([] if final else [full]),
            [charges, pbf, p, site, dots, *envs], smem=(0,), scratch=[ext_sum], flops=work)
        (sums,) = kernel_call(cross_kernel, [rows], [rim, down, dots])
        return rim, down, sums, own

    def apply(p, pbf, envs, dots, moving, counts, late=0):
        rim, down, sums, (own,) = backward(p, pbf, envs, dots)
        across = swapped(jnp.broadcast_to(sums, (4, 8, 128)), "mpo", 1)[0]
        upper = shifted(down, "sect", -1)
        chunks = [field((count, *dims), BF) for count in counts]
        first = taken[0]
        taken[0] += sum(counts)
        part, *chunks = kernel_call(
            lambda *refs: forward_kernel(first, *refs), [full, *chunks],
            [charges, rim, pbf, *envs, own, sums],
            smem=(0,), scratch=[ext], flops=work)
        own = (part + upper.astype(F32)).astype(BF)
        own, moving, chunks = lax.optimization_barrier((own, moving, chunks))
        sums = sums + across
        before.extend(moving)
        moving = [shifted(c, "sec", 1) for c in chunks[: len(chunks) - late]]
        return own, swapped(own, "mpo", 1), exchange(sums), moving, chunks[len(chunks) - late :]

    def davidson(u, ubf, dots, envs, plan, moving):
        new = [full, full, half, rows, rows]
        own, other, sums, moving, late = apply(u, ubf, envs, dots, moving, plan[0])
        x, p, pbf, st, dots, hx = kernel_call(
            lambda *refs: update_kernel(True, False, *refs), [*new, full],
            [sums, site, u, own, other])
        for turn in range(ITERS - 1):
            last = turn == ITERS - 2
            own, other, sums, moving, late = apply(
                p, pbf, envs, dots, moving, plan[1 + turn], int(last and plan[-1] != ()))
            x, p, pbf, st, dots, *hx = kernel_call(
                lambda *refs: update_kernel(False, last, *refs), new if last else [*new, full],
                [sums, site, p, own, other, x, *([hx] if turn == 0 else hx), st])
        before.extend(moving)
        sums = backward(p, pbf, envs, dots, True)[2]
        if not plan[-1]:
            return exchange(sums, ("sect", "mpo")), st, x, p
        sums = sums + swapped(sums, "mpo", 1)
        late, sums = lax.optimization_barrier((late, sums))
        before.extend(shifted(c, "sec", 1) for c in late)
        return exchange(sums), st, x, p

    u, ubf, site, dots = kernel_call(
        start_kernel, [full, half, full, rows], [counts, begin, onsite[0]], smem=(0,))
    (left_held,) = kernel_call(copy_kernel, [field(left_one.shape, BF)], [left_one])
    moving = []
    solved = davidson(u, ubf, dots, (left_held, right_one), [(2,), (2,), (2,), (3,)], moving)
    x, xbf, st_one, dots = kernel_call(
        lambda *refs: finish_kernel(False, *refs), [full, half, rows, rows], solved)
    frame = shifted(xbf, "sec", 1)
    early, _ = lax.optimization_barrier((before[:-1], xbf))
    count = sum(chunk.shape[0] for chunk in early)
    left_next, held = kernel_call(
        gather_kernel, [field(left_one.shape, BF), field((count, *dims), BF)], [left_held, *early])
    (left_next,) = kernel_call(
        lambda *refs: grow_kernel(sectors, *refs), [field(left_one.shape, BF)],
        [place, frame, left_next, held, before[-1]], smem=(0,), flops=work, alias={2: 0})
    solved = davidson(x, xbf, dots, (left_next, right_one), [()] * ITERS, [])
    x, energies = kernel_call(
        lambda *refs: finish_kernel(True, *refs), [full, field((1, 2), F32)], [*solved, st_one])
    return x[None], energies


def solution(mesh):
    return jax.shard_map(
        on_device,
        mesh=mesh,
        in_specs=(
            P("sec", "mpo", "sect", None, None),
            P("sec", "mpo", "sect", None, None),
            P("sec", "sect", None, None),
            P("sec", "sect", None, None),
            P("mpo"),
            P("sec", None, "sect"),
        ),
        out_specs=(P("sec", "sect", None, None), P("sec", None)),
        check_vma=False,
    )
```

```python
import math

import jax
import jax.numpy as jnp
from jax import lax
from jax.experimental import pallas as pl
from jax.experimental.pallas import tpu as pltpu
from jax.sharding import PartitionSpec as P

CHARGE_MAX = 2
ITERS = 4
ROWS = 64

BF = jnp.bfloat16
F32 = jnp.float32


def shifted(x, axis, by):
    size = lax.axis_size(axis)
    pairs = [(i, i + by) for i in range(size) if 0 <= i + by < size]
    return lax.ppermute(x, axis, pairs)


def swapped(x, axis, mask):
    return lax.ppermute(x, axis, [(i, i ^ mask) for i in range(lax.axis_size(axis))])


def dot(a, b):
    return jnp.dot(a, b, preferred_element_type=F32)


def kernel_call(body, outs, operands, smem=(), scratch=(), vmem=12, flops=0, alias=None):
    spaces = [pltpu.SMEM if k in smem else pltpu.VMEM for k in range(len(operands))]
    return pl.pallas_call(
        body,
        out_shape=outs,
        in_specs=[pl.BlockSpec(memory_space=space) for space in spaces],
        out_specs=[pl.BlockSpec(memory_space=pltpu.VMEM)] * len(outs),
        scratch_shapes=list(scratch),
        input_output_aliases=alias or {},
        compiler_params=pltpu.CompilerParams(vmem_limit_bytes=vmem * 2**20),
        cost_estimate=pl.CostEstimate(flops=flops, bytes_accessed=4 * 2**20, transcendentals=0),
    )(*operands)


def field(dims, kind):
    return jax.ShapeDtypeStruct(dims, kind)


def chunk_mask(counts_ref, sector, first_row, block):
    rows = lax.broadcasted_iota(jnp.int32, (ROWS, block), 0) + first_row
    cols = lax.broadcasted_iota(jnp.int32, (ROWS, block), 1)
    return (rows < counts_ref[0, sector]) & (cols < counts_ref[1, sector])


def chunks(sec_dev, block, step, init):
    per = block // ROWS

    def body(k, carry):
        return step(k // per, pl.ds(pl.multiple_of((k % per) * ROWS, ROWS), ROWS), (k % per) * ROWS, carry)

    return lax.fori_loop(0, sec_dev * per, body, init)


def fold(values):
    rows, cols = values.shape
    return jnp.sum(values.reshape(rows // 8, 8, cols), axis=0)


def lanes(acc):
    row = jnp.sum(acc, axis=0, keepdims=True)
    total = row[:, :128]
    for k in range(1, row.shape[1] // 128):
        total = total + row[:, 128 * k : 128 * (k + 1)]
    return total


def write_rows(out_ref, rows):
    index = lax.broadcasted_iota(jnp.int32, (8, 128), 0)
    total = jnp.zeros((8, 128), F32)
    for k, row in enumerate(rows):
        if row is not None:
            total = jnp.where(index == k, jnp.broadcast_to(row, (8, 128)), total)
    out_ref[...] = total


def read_sums(sums_ref):
    total = jnp.sum(jnp.sum(sums_ref[...], axis=0), axis=1, keepdims=True)
    return [total[k : k + 1, :] for k in range(5)]


def rotation(sums, theta):
    pp_ham, xp, pp, hxp, xx = sums
    length = jnp.sqrt(pp - 2.0 * xp * xp + xp * xp * xx)
    cross = (hxp - xp * theta) / length
    curv = (pp_ham - 2.0 * xp * hxp + xp * xp * theta) / (length * length)
    two_b, diff = 2.0 * cross, theta - curv
    radius = jnp.sqrt(two_b * two_b + diff * diff)
    flat = radius == 0.0
    cos_full = jnp.where(flat, 1.0, diff / jnp.where(flat, 1.0, radius))
    sin_full = jnp.where(flat, 0.0, jnp.abs(two_b) / jnp.where(flat, 1.0, radius))
    major = jnp.sqrt(0.5 * (1.0 + jnp.abs(cos_full)))
    minor = 0.5 * sin_full / major
    weight_x = jnp.where(cos_full >= 0.0, minor, major)
    weight_t = jnp.where(cos_full >= 0.0, major, minor)
    weight_t = jnp.where(two_b > 0.0, -weight_t, weight_t)
    theta_new = (
        weight_x * weight_x * theta
        + 2.0 * weight_x * weight_t * cross
        + weight_t * weight_t * curv
    )
    coef_p = weight_t / length
    return weight_x - coef_p * xp, coef_p, theta_new


def start_kernel(counts_ref, begin_ref, site_ref, u_ref, ubf_ref, signed_ref, dots_ref):
    sec_dev, block, _ = u_ref.shape

    def step(s, rows, first, acc):
        kept = chunk_mask(counts_ref, s, first, block)
        site = site_ref[s, rows, :]
        u = jnp.where(kept, begin_ref[s, rows, :], 0.0)
        signed_ref[s, rows, :] = jnp.where(kept, site, -site)
        u_ref[s, rows, :] = u
        ubf_ref[s, rows, :] = u.astype(BF)
        return acc + fold(u * u)

    acc = chunks(sec_dev, block, step, jnp.zeros((8, block), F32))
    write_rows(dots_ref, [None, None, 0.5 * lanes(acc)])


def update_kernel(first_step, last_step, *refs):
    if first_step:
        sums_ref, site_ref, p_ref, own_ref, other_ref, *outs = refs
    else:
        sums_ref, site_ref, p_ref, own_ref, other_ref, x_ref, hx_ref, st_ref, *outs = refs
    xn_ref, pn_ref, pbf_ref, stn_ref, dots_ref, *hxn_ref = outs
    sec_dev, block, _ = p_ref.shape
    sums = read_sums(sums_ref)
    if first_step:
        theta = sums[0] / sums[2]
        coef_p = 1.0 / jnp.sqrt(sums[2])
    else:
        coef_x, coef_p, theta = rotation(sums, st_ref[0:1, 0:1])
    stn_ref[...] = jnp.broadcast_to(theta, stn_ref.shape)

    def step(s, rows, first, acc):
        p = p_ref[s, rows, :]
        site = site_ref[s, rows, :]
        image = own_ref[s, rows, :].astype(F32) + other_ref[s, rows, :].astype(F32) + site * p
        image = jnp.where(site > 0.0, image, 0.0)
        if first_step:
            x, hx = coef_p * p, coef_p * image
        else:
            x = coef_x * x_ref[s, rows, :] + coef_p * p
            hx = coef_x * hx_ref[s, rows, :] + coef_p * image
        new = (hx - theta * x) / jnp.maximum(jnp.abs(site - theta), 1.0)
        xn_ref[s, rows, :] = x
        if not last_step:
            hxn_ref[0][s, rows, :] = hx
        pn_ref[s, rows, :] = new
        pbf_ref[s, rows, :] = new.astype(BF)
        return (
            acc[0] + fold(x * new),
            acc[1] + fold(new * new),
            acc[2] + fold(hx * new),
            acc[3] + fold(x * x),
        )

    zero = jnp.zeros((8, block), F32)
    acc = chunks(sec_dev, block, step, (zero, zero, zero, zero))
    write_rows(dots_ref, [None] + [0.5 * lanes(a) for a in acc])


def finish_kernel(last, sums_ref, st_ref, x_ref, p_ref, *refs):
    if last:
        st_one_ref, xn_ref, stn_ref = refs
    else:
        xn_ref, xbf_ref, stn_ref, dots_ref = refs
    sec_dev, block, _ = p_ref.shape
    coef_x, coef_p, theta = rotation(read_sums(sums_ref), st_ref[0:1, 0:1])
    if last:
        stn_ref[...] = jnp.concatenate([st_one_ref[0:1, 0:1], theta], axis=1)
    else:
        stn_ref[...] = jnp.broadcast_to(theta, stn_ref.shape)

    def step(s, rows, first, acc):
        x = coef_x * x_ref[s, rows, :] + coef_p * p_ref[s, rows, :]
        xn_ref[s, rows, :] = x
        if not last:
            xbf_ref[s, rows, :] = x.astype(BF)
            acc = acc + fold(x * x)
        return acc

    acc = chunks(sec_dev, block, step, jnp.zeros((8, block), F32))
    if not last:
        write_rows(dots_ref, [None, None, 0.5 * lanes(acc)])


def adjoint_kernel(
    charges_ref, pbf_ref, p_ref, site_ref, dots_ref, left_ref, right_ref, down_ref, sums_ref, *refs
):
    *own_ref, acc_ref = refs
    terms, sec_dev, block, _ = left_ref.shape
    acc_ref[...] = jnp.zeros_like(acc_ref)
    for s in range(sec_dev):
        turned = pbf_ref[s].T
        for w in range(terms):
            adjoint = dot(turned, left_ref[w, s]).astype(BF)
            target = s + CHARGE_MAX - charges_ref[w]
            acc_ref[target] += dot(right_ref[w, s], adjoint)
    total = jnp.zeros((8, block), F32)
    for s in range(sec_dev):
        down_ref[s] = acc_ref[s].T.astype(BF)
        own = acc_ref[CHARGE_MAX + s].T
        if own_ref:
            own_ref[0][s] = own
        p = p_ref[s]
        total = total + fold(p * (2.0 * own + 0.5 * site_ref[s] * p))
    index = lax.broadcasted_iota(jnp.int32, (8, 128), 0)
    row = jnp.broadcast_to(lanes(total), (8, 128))
    sums_ref[...] = jnp.where(index == 0, row, dots_ref[...])


def cross_kernel(rim_ref, down_ref, dots_ref, sums_ref):
    sec_dev, block, _ = rim_ref.shape

    def step(s, rows, first, acc):
        return acc + fold(rim_ref[s, rows, :].astype(F32) * down_ref[s, rows, :].astype(F32))

    acc = chunks(sec_dev, block, step, jnp.zeros((8, block), F32))
    index = lax.broadcasted_iota(jnp.int32, (8, 128), 0)
    row = jnp.broadcast_to(2.0 * lanes(acc), (8, 128))
    sums_ref[...] = dots_ref[...] + jnp.where(index == 0, row, 0.0)


def forward_kernel(
    first, charges_ref, rim_ref, pbf_ref, left_ref, right_ref, own_ref, after_ref,
    part_ref, *refs,
):
    *chunk_refs, ext_ref = refs
    terms, sec_dev, block, _ = left_ref.shape
    for chunk_ref in chunk_refs:
        chunk_ref[...] = left_ref[first : first + chunk_ref.shape[0]]
        first += chunk_ref.shape[0]
    ext_ref[:CHARGE_MAX] = rim_ref[...]
    ext_ref[CHARGE_MAX:] = pbf_ref[...]
    for s in range(sec_dev):
        out = own_ref[s]
        for w in range(terms):
            moved = ext_ref[s + CHARGE_MAX - charges_ref[w]]
            inner = dot(left_ref[w, s], moved).astype(BF)
            out = out + dot(inner, right_ref[w, s])
        part_ref[s] = out


def gather_kernel(*refs):
    left_ref, *before_refs, next_ref, held_ref = refs
    next_ref[...] = left_ref[...]
    first = 0
    for ref in before_refs:
        held_ref[first : first + ref.shape[0]] = ref[...]
        first += ref.shape[0]


def grow_kernel(sectors, place_ref, frame_ref, next_ref, *refs):
    *before_refs, out_ref = refs
    _, sec_dev, block, _ = next_ref.shape
    scale = math.sqrt(sectors * block)

    @pl.when(place_ref[0] == 0)
    def _():
        out_ref[...] = next_ref[...]

    slots = [ref.at[k] for ref in before_refs for k in range(ref.shape[0])]

    @pl.when(place_ref[0] != 0)
    def _():
        for s in range(sec_dev):
            frame = (frame_ref[s].astype(F32) * scale).astype(BF)
            turned = frame.T
            for w, slot in enumerate(slots):
                half = dot(turned, slot[s]).astype(BF)
                out_ref[w, s] = dot(half, frame).astype(BF)


def copy_kernel(in_ref, out_ref, chunk_ref):
    out_ref[...] = in_ref[...]
    chunk_ref[...] = in_ref[: chunk_ref.shape[0]]


def on_device(left_env, right_env, onsite, initial, charges, kept_counts):
    left_one, right_one = left_env[0], right_env[0]
    begin, counts = initial[0], kept_counts[0]
    terms, sec_dev, block, _ = left_one.shape
    dims = (sec_dev, block, block)
    full, half, rows = field(dims, F32), field(dims, BF), field((8, 128), F32)
    work = 4 * terms * sec_dev * block**3
    place = lax.axis_index("sec").astype(jnp.int32).reshape(1)
    peers = lax.axis_size("sect")
    sectors = sec_dev * peers
    ext = pltpu.VMEM((sec_dev + CHARGE_MAX, block, block), BF)
    ext_sum = pltpu.VMEM((sec_dev + CHARGE_MAX, block, block), F32)
    before = []
    taken = [0]

    def exchange(sums, axes="sect"):
        count = math.prod(lax.axis_size(axis) for axis in ([axes] if axes == "sect" else axes))
        return lax.all_to_all(jnp.broadcast_to(sums, (count, 8, 128)), axes, 0, 0)

    def backward(p, pbf, envs, dots, final=False):
        rim = shifted(pbf, "sect", 1)
        down, dots, *own = kernel_call(
            adjoint_kernel, [half, rows] + ([] if final else [full]),
            [charges, pbf, p, site, dots, *envs], smem=(0,), scratch=[ext_sum], flops=work)
        (sums,) = kernel_call(cross_kernel, [rows], [rim, down, dots])
        return rim, down, sums, own

    def apply(p, pbf, envs, dots, moving, counts, late=0):
        rim, down, sums, (own,) = backward(p, pbf, envs, dots)
        across = swapped(jnp.broadcast_to(sums, (4, 8, 128)), "mpo", 1)[0]
        upper = shifted(down, "sect", -1)
        chunks = [field((count, *dims), BF) for count in counts]
        first = taken[0]
        taken[0] += sum(counts)
        part, *chunks = kernel_call(
            lambda *refs: forward_kernel(first, *refs), [full, *chunks],
            [charges, rim, pbf, *envs, own, sums],
            smem=(0,), scratch=[ext], flops=work)
        own = (part + upper.astype(F32)).astype(BF)
        own, moving, chunks = lax.optimization_barrier((own, moving, chunks))
        sums = sums + across
        before.extend(moving)
        moving = [shifted(c, "sec", 1) for c in chunks[: len(chunks) - late]]
        return own, swapped(own, "mpo", 1), exchange(sums), moving, chunks[len(chunks) - late :]

    def davidson(u, ubf, dots, envs, plan, moving):
        new = [full, full, half, rows, rows]
        own, other, sums, moving, late = apply(u, ubf, envs, dots, moving, plan[0])
        x, p, pbf, st, dots, hx = kernel_call(
            lambda *refs: update_kernel(True, False, *refs), [*new, full],
            [sums, site, u, own, other])
        for turn in range(ITERS - 1):
            last = turn == ITERS - 2
            own, other, sums, moving, late = apply(
                p, pbf, envs, dots, moving, plan[1 + turn], int(last and plan[-1] != ()))
            x, p, pbf, st, dots, *hx = kernel_call(
                lambda *refs: update_kernel(False, last, *refs), new if last else [*new, full],
                [sums, site, p, own, other, x, *([hx] if turn == 0 else hx), st])
        before.extend(moving)
        sums = backward(p, pbf, envs, dots, True)[2]
        if not plan[-1]:
            return exchange(sums, ("sect", "mpo")), st, x, p
        sums = sums + swapped(sums, "mpo", 1)
        late, sums = lax.optimization_barrier((late, sums))
        before.extend(shifted(c, "sec", 1) for c in late)
        return exchange(sums), st, x, p

    u, ubf, site, dots = kernel_call(
        start_kernel, [full, half, full, rows], [counts, begin, onsite[0]], smem=(0,))
    left_held, chunk = kernel_call(
        copy_kernel, [field(left_one.shape, BF), field((3, *dims), BF)], [left_one])
    taken[0] = 3
    moving = [shifted(chunk, "sec", 1)]
    solved = davidson(u, ubf, dots, (left_held, right_one), [(2,), (), (2,), (2,)], moving)
    x, xbf, st_one, dots = kernel_call(
        lambda *refs: finish_kernel(False, *refs), [full, half, rows, rows], solved)
    frame = shifted(xbf, "sec", 1)
    early, _ = lax.optimization_barrier((before[:-1], xbf))
    count = sum(chunk.shape[0] for chunk in early)
    left_next, held = kernel_call(
        gather_kernel, [field(left_one.shape, BF), field((count, *dims), BF)], [left_held, *early])
    (left_next,) = kernel_call(
        lambda *refs: grow_kernel(sectors, *refs), [field(left_one.shape, BF)],
        [place, frame, left_next, held, before[-1]], smem=(0,), flops=work, alias={2: 0})
    solved = davidson(x, xbf, dots, (left_next, right_one), [()] * ITERS, [])
    x, energies = kernel_call(
        lambda *refs: finish_kernel(True, *refs), [full, field((1, 2), F32)], [*solved, st_one])
    return x[None], energies


def solution(mesh):
    return jax.shard_map(
        on_device,
        mesh=mesh,
        in_specs=(
            P("sec", "mpo", "sect", None, None),
            P("sec", "mpo", "sect", None, None),
            P("sec", "sect", None, None),
            P("sec", "sect", None, None),
            P("mpo"),
            P("sec", None, "sect"),
        ),
        out_specs=(P("sec", "sect", None, None), P("sec", None)),
        check_vma=False,
    )
```

```python
import math

import jax
import jax.numpy as jnp
from jax import lax
from jax.experimental import pallas as pl
from jax.experimental.pallas import tpu as pltpu
from jax.sharding import PartitionSpec as P

CHARGE_MAX = 2
ITERS = 4
ROWS = 64

BF = jnp.bfloat16
F32 = jnp.float32


def shifted(x, axis, by):
    size = lax.axis_size(axis)
    pairs = [(i, i + by) for i in range(size) if 0 <= i + by < size]
    return lax.ppermute(x, axis, pairs)


def swapped(x, axis, mask):
    return lax.ppermute(x, axis, [(i, i ^ mask) for i in range(lax.axis_size(axis))])


def dot(a, b):
    return jnp.dot(a, b, preferred_element_type=F32)


def kernel_call(body, outs, operands, smem=(), scratch=(), vmem=12, flops=0, alias=None):
    spaces = [pltpu.SMEM if k in smem else pltpu.VMEM for k in range(len(operands))]
    return pl.pallas_call(
        body,
        out_shape=outs,
        in_specs=[pl.BlockSpec(memory_space=space) for space in spaces],
        out_specs=[pl.BlockSpec(memory_space=pltpu.VMEM)] * len(outs),
        scratch_shapes=list(scratch),
        input_output_aliases=alias or {},
        compiler_params=pltpu.CompilerParams(vmem_limit_bytes=vmem * 2**20),
        cost_estimate=pl.CostEstimate(flops=flops, bytes_accessed=4 * 2**20, transcendentals=0),
    )(*operands)


def field(dims, kind):
    return jax.ShapeDtypeStruct(dims, kind)


def chunk_mask(counts_ref, sector, first_row, block):
    rows = lax.broadcasted_iota(jnp.int32, (ROWS, block), 0) + first_row
    cols = lax.broadcasted_iota(jnp.int32, (ROWS, block), 1)
    return (rows < counts_ref[0, sector]) & (cols < counts_ref[1, sector])


def chunks(sec_dev, block, step, init):
    per = block // ROWS

    def body(k, carry):
        return step(k // per, pl.ds(pl.multiple_of((k % per) * ROWS, ROWS), ROWS), (k % per) * ROWS, carry)

    return lax.fori_loop(0, sec_dev * per, body, init)


def fold(values):
    rows, cols = values.shape
    return jnp.sum(values.reshape(rows // 8, 8, cols), axis=0)


def lanes(acc):
    row = jnp.sum(acc, axis=0, keepdims=True)
    total = row[:, :128]
    for k in range(1, row.shape[1] // 128):
        total = total + row[:, 128 * k : 128 * (k + 1)]
    return total


def write_rows(out_ref, rows):
    index = lax.broadcasted_iota(jnp.int32, (8, 128), 0)
    total = jnp.zeros((8, 128), F32)
    for k, row in enumerate(rows):
        if row is not None:
            total = jnp.where(index == k, jnp.broadcast_to(row, (8, 128)), total)
    out_ref[...] = total


def read_sums(sums_ref):
    total = jnp.sum(jnp.sum(sums_ref[...], axis=0), axis=1, keepdims=True)
    return [total[k : k + 1, :] for k in range(5)]


def rotation(sums, theta):
    pp_ham, xp, pp, hxp, xx = sums
    length = jnp.sqrt(pp - 2.0 * xp * xp + xp * xp * xx)
    cross = (hxp - xp * theta) / length
    curv = (pp_ham - 2.0 * xp * hxp + xp * xp * theta) / (length * length)
    two_b, diff = 2.0 * cross, theta - curv
    radius = jnp.sqrt(two_b * two_b + diff * diff)
    flat = radius == 0.0
    cos_full = jnp.where(flat, 1.0, diff / jnp.where(flat, 1.0, radius))
    sin_full = jnp.where(flat, 0.0, jnp.abs(two_b) / jnp.where(flat, 1.0, radius))
    major = jnp.sqrt(0.5 * (1.0 + jnp.abs(cos_full)))
    minor = 0.5 * sin_full / major
    weight_x = jnp.where(cos_full >= 0.0, minor, major)
    weight_t = jnp.where(cos_full >= 0.0, major, minor)
    weight_t = jnp.where(two_b > 0.0, -weight_t, weight_t)
    theta_new = (
        weight_x * weight_x * theta
        + 2.0 * weight_x * weight_t * cross
        + weight_t * weight_t * curv
    )
    coef_p = weight_t / length
    return weight_x - coef_p * xp, coef_p, theta_new


def start_kernel(counts_ref, begin_ref, site_ref, u_ref, ubf_ref, signed_ref, dots_ref):
    sec_dev, block, _ = u_ref.shape

    def step(s, rows, first, acc):
        kept = chunk_mask(counts_ref, s, first, block)
        site = site_ref[s, rows, :]
        u = jnp.where(kept, begin_ref[s, rows, :], 0.0)
        signed_ref[s, rows, :] = jnp.where(kept, site, -site)
        u_ref[s, rows, :] = u
        ubf_ref[s, rows, :] = u.astype(BF)
        return acc + fold(u * u)

    acc = chunks(sec_dev, block, step, jnp.zeros((8, block), F32))
    write_rows(dots_ref, [None, None, 0.5 * lanes(acc)])


def update_kernel(first_step, last_step, *refs):
    if first_step:
        sums_ref, site_ref, p_ref, own_ref, other_ref, *outs = refs
    else:
        sums_ref, site_ref, p_ref, own_ref, other_ref, x_ref, hx_ref, st_ref, *outs = refs
    xn_ref, pn_ref, pbf_ref, stn_ref, dots_ref, *hxn_ref = outs
    sec_dev, block, _ = p_ref.shape
    sums = read_sums(sums_ref)
    if first_step:
        theta = sums[0] / sums[2]
        coef_p = 1.0 / jnp.sqrt(sums[2])
    else:
        coef_x, coef_p, theta = rotation(sums, st_ref[0:1, 0:1])
    stn_ref[...] = jnp.broadcast_to(theta, stn_ref.shape)

    def step(s, rows, first, acc):
        p = p_ref[s, rows, :]
        site = site_ref[s, rows, :]
        image = own_ref[s, rows, :].astype(F32) + other_ref[s, rows, :].astype(F32) + site * p
        image = jnp.where(site > 0.0, image, 0.0)
        if first_step:
            x, hx = coef_p * p, coef_p * image
        else:
            x = coef_x * x_ref[s, rows, :] + coef_p * p
            hx = coef_x * hx_ref[s, rows, :] + coef_p * image
        new = (hx - theta * x) / jnp.maximum(jnp.abs(site - theta), 1.0)
        xn_ref[s, rows, :] = x
        if not last_step:
            hxn_ref[0][s, rows, :] = hx
        pn_ref[s, rows, :] = new
        pbf_ref[s, rows, :] = new.astype(BF)
        return (
            acc[0] + fold(x * new),
            acc[1] + fold(new * new),
            acc[2] + fold(hx * new),
            acc[3] + fold(x * x),
        )

    zero = jnp.zeros((8, block), F32)
    acc = chunks(sec_dev, block, step, (zero, zero, zero, zero))
    write_rows(dots_ref, [None] + [0.5 * lanes(a) for a in acc])


def finish_kernel(last, sums_ref, st_ref, x_ref, p_ref, *refs):
    if last:
        st_one_ref, xn_ref, stn_ref = refs
    else:
        xn_ref, xbf_ref, stn_ref, dots_ref = refs
    sec_dev, block, _ = p_ref.shape
    coef_x, coef_p, theta = rotation(read_sums(sums_ref), st_ref[0:1, 0:1])
    if last:
        stn_ref[...] = jnp.concatenate([st_one_ref[0:1, 0:1], theta], axis=1)
    else:
        stn_ref[...] = jnp.broadcast_to(theta, stn_ref.shape)

    def step(s, rows, first, acc):
        x = coef_x * x_ref[s, rows, :] + coef_p * p_ref[s, rows, :]
        xn_ref[s, rows, :] = x
        if not last:
            xbf_ref[s, rows, :] = x.astype(BF)
            acc = acc + fold(x * x)
        return acc

    acc = chunks(sec_dev, block, step, jnp.zeros((8, block), F32))
    if not last:
        write_rows(dots_ref, [None, None, 0.5 * lanes(acc)])


def adjoint_kernel(
    charges_ref, pbf_ref, p_ref, site_ref, dots_ref, left_ref, right_ref, down_ref, sums_ref, *refs
):
    *own_ref, acc_ref = refs
    terms, sec_dev, block, _ = left_ref.shape
    acc_ref[...] = jnp.zeros_like(acc_ref)
    for s in range(sec_dev):
        turned = pbf_ref[s].T
        for w in range(terms):
            adjoint = dot(turned, left_ref[w, s]).astype(BF)
            target = s + CHARGE_MAX - charges_ref[w]
            acc_ref[target] += dot(right_ref[w, s], adjoint)
    total = jnp.zeros((8, block), F32)
    for s in range(sec_dev):
        down_ref[s] = acc_ref[s].T.astype(BF)
        own = acc_ref[CHARGE_MAX + s].T
        if own_ref:
            own_ref[0][s] = own
        p = p_ref[s]
        total = total + fold(p * (2.0 * own + 0.5 * site_ref[s] * p))
    index = lax.broadcasted_iota(jnp.int32, (8, 128), 0)
    row = jnp.broadcast_to(lanes(total), (8, 128))
    sums_ref[...] = jnp.where(index == 0, row, dots_ref[...])


def cross_kernel(rim_ref, down_ref, dots_ref, sums_ref):
    sec_dev, block, _ = rim_ref.shape

    def step(s, rows, first, acc):
        return acc + fold(rim_ref[s, rows, :].astype(F32) * down_ref[s, rows, :].astype(F32))

    acc = chunks(sec_dev, block, step, jnp.zeros((8, block), F32))
    index = lax.broadcasted_iota(jnp.int32, (8, 128), 0)
    row = jnp.broadcast_to(2.0 * lanes(acc), (8, 128))
    sums_ref[...] = dots_ref[...] + jnp.where(index == 0, row, 0.0)


def forward_kernel(
    first, charges_ref, rim_ref, pbf_ref, left_ref, right_ref, own_ref, after_ref,
    part_ref, *refs,
):
    *chunk_refs, ext_ref = refs
    terms, sec_dev, block, _ = left_ref.shape
    for chunk_ref in chunk_refs:
        chunk_ref[...] = left_ref[first : first + chunk_ref.shape[0]]
        first += chunk_ref.shape[0]
    ext_ref[:CHARGE_MAX] = rim_ref[...]
    ext_ref[CHARGE_MAX:] = pbf_ref[...]
    for s in range(sec_dev):
        out = own_ref[s]
        for w in range(terms):
            moved = ext_ref[s + CHARGE_MAX - charges_ref[w]]
            inner = dot(left_ref[w, s], moved).astype(BF)
            out = out + dot(inner, right_ref[w, s])
        part_ref[s] = out


def gather_kernel(*refs):
    left_ref, *before_refs, next_ref, held_ref = refs
    next_ref[...] = left_ref[...]
    first = 0
    for ref in before_refs:
        held_ref[first : first + ref.shape[0]] = ref[...]
        first += ref.shape[0]


def grow_kernel(sectors, place_ref, frame_ref, next_ref, *refs):
    *before_refs, out_ref = refs
    _, sec_dev, block, _ = next_ref.shape
    scale = math.sqrt(sectors * block)

    @pl.when(place_ref[0] == 0)
    def _():
        out_ref[...] = next_ref[...]

    slots = [ref.at[k] for ref in before_refs for k in range(ref.shape[0])]

    @pl.when(place_ref[0] != 0)
    def _():
        for s in range(sec_dev):
            frame = (frame_ref[s].astype(F32) * scale).astype(BF)
            turned = frame.T
            for w, slot in enumerate(slots):
                half = dot(turned, slot[s]).astype(BF)
                out_ref[w, s] = dot(half, frame).astype(BF)


def copy_kernel(in_ref, out_ref, chunk_ref):
    out_ref[...] = in_ref[...]
    chunk_ref[...] = in_ref[: chunk_ref.shape[0]]


def on_device(left_env, right_env, onsite, initial, charges, kept_counts):
    left_one, right_one = left_env[0], right_env[0]
    begin, counts = initial[0], kept_counts[0]
    terms, sec_dev, block, _ = left_one.shape
    dims = (sec_dev, block, block)
    full, half, rows = field(dims, F32), field(dims, BF), field((8, 128), F32)
    work = 4 * terms * sec_dev * block**3
    place = lax.axis_index("sec").astype(jnp.int32).reshape(1)
    peers = lax.axis_size("sect")
    sectors = sec_dev * peers
    ext = pltpu.VMEM((sec_dev + CHARGE_MAX, block, block), BF)
    ext_sum = pltpu.VMEM((sec_dev + CHARGE_MAX, block, block), F32)
    before = []
    taken = [0]

    def exchange(sums, axes="sect"):
        count = math.prod(lax.axis_size(axis) for axis in ([axes] if axes == "sect" else axes))
        return lax.all_to_all(jnp.broadcast_to(sums, (count, 8, 128)), axes, 0, 0)

    def backward(p, pbf, envs, dots, final=False):
        rim = shifted(pbf, "sect", 1)
        down, dots, *own = kernel_call(
            adjoint_kernel, [half, rows] + ([] if final else [full]),
            [charges, pbf, p, site, dots, *envs], smem=(0,), scratch=[ext_sum], flops=work)
        (sums,) = kernel_call(cross_kernel, [rows], [rim, down, dots])
        return rim, down, sums, own

    def apply(p, pbf, envs, dots, moving, counts, late=0):
        rim, down, sums, (own,) = backward(p, pbf, envs, dots)
        across = swapped(jnp.broadcast_to(sums, (4, 8, 128)), "mpo", 1)[0]
        upper = shifted(down, "sect", -1)
        chunks = [field((count, *dims), BF) for count in counts]
        first = taken[0]
        taken[0] += sum(counts)
        part, *chunks = kernel_call(
            lambda *refs: forward_kernel(first, *refs), [full, *chunks],
            [charges, rim, pbf, *envs, own, sums],
            smem=(0,), scratch=[ext], flops=work)
        own = (part + upper.astype(F32)).astype(BF)
        own, moving, chunks = lax.optimization_barrier((own, moving, chunks))
        sums = sums + across
        before.extend(moving)
        moving = [shifted(c, "sec", 1) for c in chunks[: len(chunks) - late]]
        return own, swapped(own, "mpo", 1), exchange(sums), moving, chunks[len(chunks) - late :]

    def davidson(u, ubf, dots, envs, plan, moving):
        new = [full, full, half, rows, rows]
        own, other, sums, moving, late = apply(u, ubf, envs, dots, moving, plan[0])
        x, p, pbf, st, dots, hx = kernel_call(
            lambda *refs: update_kernel(True, False, *refs), [*new, full],
            [sums, site, u, own, other])
        for turn in range(ITERS - 1):
            last = turn == ITERS - 2
            own, other, sums, moving, late = apply(
                p, pbf, envs, dots, moving, plan[1 + turn], int(last and plan[-1] != ()))
            x, p, pbf, st, dots, *hx = kernel_call(
                lambda *refs: update_kernel(False, last, *refs), new if last else [*new, full],
                [sums, site, p, own, other, x, *([hx] if turn == 0 else hx), st])
        before.extend(moving)
        sums = backward(p, pbf, envs, dots, True)[2]
        if not plan[-1]:
            return exchange(sums, ("sect", "mpo")), st, x, p
        sums = sums + swapped(sums, "mpo", 1)
        late, sums = lax.optimization_barrier((late, sums))
        before.extend(shifted(c, "sec", 1) for c in late)
        return exchange(sums), st, x, p

    u, ubf, site, dots = kernel_call(
        start_kernel, [full, half, full, rows], [counts, begin, onsite[0]], smem=(0,))
    left_held, chunk = kernel_call(
        copy_kernel, [field(left_one.shape, BF), field((3, *dims), BF)], [left_one])
    taken[0] = 3
    chunk, ubf = lax.optimization_barrier((chunk, ubf))
    moving = [shifted(chunk, "sec", 1)]
    solved = davidson(u, ubf, dots, (left_held, right_one), [(2,), (), (2,), (2,)], moving)
    x, xbf, st_one, dots = kernel_call(
        lambda *refs: finish_kernel(False, *refs), [full, half, rows, rows], solved)
    frame = shifted(xbf, "sec", 1)
    early, _ = lax.optimization_barrier((before[:-1], xbf))
    count = sum(chunk.shape[0] for chunk in early)
    left_next, held = kernel_call(
        gather_kernel, [field(left_one.shape, BF), field((count, *dims), BF)], [left_held, *early])
    (left_next,) = kernel_call(
        lambda *refs: grow_kernel(sectors, *refs), [field(left_one.shape, BF)],
        [place, frame, left_next, held, before[-1]], smem=(0,), flops=work, alias={2: 0})
    solved = davidson(x, xbf, dots, (left_next, right_one), [()] * ITERS, [])
    x, energies = kernel_call(
        lambda *refs: finish_kernel(True, *refs), [full, field((1, 2), F32)], [*solved, st_one])
    return x[None], energies


def solution(mesh):
    return jax.shard_map(
        on_device,
        mesh=mesh,
        in_specs=(
            P("sec", "mpo", "sect", None, None),
            P("sec", "mpo", "sect", None, None),
            P("sec", "sect", None, None),
            P("sec", "sect", None, None),
            P("mpo"),
            P("sec", None, "sect"),
        ),
        out_specs=(P("sec", "sect", None, None), P("sec", None)),
        check_vma=False,
    )
```
